32 devices in a mesh: grp: 2 (over y), sx: 4 (over x, core), sy: 4 (over z).
Axes of the slice: x: 2, y: 2, z: 4, core: 2. Of those that a mesh axis runs over, the one named last changes fastest.
Arguments:
- probes: float32 [64, 16, 8, 128], P('grp', 'sx', 'sy'), parts along dimension 0, may hold values from -6 to 6
- lowrank_factor: bfloat16 [32, 8, 128, 4096], P(('grp', 'sx'), 'sy'), parts along dimension 0, may hold values from -0.09375 to 0.09375
- taper_blocks: bfloat16 [32, 8, 5, 128, 128], P(('grp', 'sx'), 'sy'), parts along dimension 0, may hold values from -0.03515625 to 0.03515625
- taper_mask: int32 [32, 8, 5], P(('grp', 'sx'), 'sy'), parts along dimension 0, may hold values 0 or 1
- nugget: float32 [32, 8, 128], P(('grp', 'sx'), 'sy'), parts along dimension 0, may hold values from 1.5 to 6
Outputs:
- solution: float32 [64, 16, 8, 128], P('grp', 'sx', 'sy'), parts along dimension 0
- remainder: float32 [64, 16, 8, 128], P('grp', 'sx', 'sy'), parts along dimension 0
- gradient: float32 [2], P('grp'), parts along dimension 0
The draws below stay inside these ranges and needn't reach their ends.
There are 2 independent parts, one for each index of `grp`. The reference program is written for one: setup_inputs(seed, part) draws one part's arguments, and reference() takes and returns one part's arrays. A program takes and returns all parts, laid end to end along the dimension named above; each array names one. Nothing has to cross between parts.
All inputs are finite; a program needn't handle non-finite values. No bound on the sum of `taper_mask` on one device may be relied on, other than what follows from the above.
Results may differ from the reference program's by a relative error of at most 0.0061.
Values may be sent and summed in bfloat16 or wider, within the bound.
A program may use at most 64 MiB of HBM per device.

```python
import math
import jax
import jax.numpy as jnp
from jax import lax

S = 128
M = 4096
K = 32
ITERS = 2
TX = 16
TY = 8


def set_ends(drawn, key, least, largest):
    index_at = [jax.random.randint(jax.random.fold_in(key, axis), (), 0, length) for axis, length in enumerate(drawn.shape)]
    widest = drawn.shape.index(max(drawn.shape))
    beside = index_at[:widest] + [(index_at[widest] + 1) % drawn.shape[widest]] + index_at[widest + 1:]
    return drawn.at[tuple(index_at)].set(least).at[tuple(beside)].set(largest)


def level_of(rng, dims, split, low, high):
    gain, own = 1.0, jax.random.fold_in(rng, 6)
    for dim, parts in split:
        heights = jnp.exp(jax.random.uniform(jax.random.fold_in(own, dim), (parts,), jnp.float32, low / len(split), high / len(split)))
        gain = gain * jnp.repeat(heights, dims[dim] // parts).reshape([-1 if axis == dim else 1 for axis in range(len(dims))])
    return gain


def bell_draw(stream_key, extent, spread, limit, split=(), kind=jnp.bfloat16):
    result = spread * jax.random.normal(stream_key, extent, jnp.float32)
    if split:
        result = result * level_of(stream_key, extent, split, -0.22, 0.18)
    return jnp.clip(result, -limit, limit).astype(kind)


def setup_inputs(seed: int = 0, part: int = 0) -> dict:
    key_of = jax.random.split(jax.random.key(seed), 6)
    own_keys = jax.random.split(jax.random.fold_in(key_of[5], part), 6)
    probes = bell_draw(own_keys[0], (K, TX, TY, S), 1.0, 6.0, ((1, 4), (2, 4)), jnp.float32)
    lowrank_factor = bell_draw(own_keys[1], (TX, TY, S, M), M ** -0.5, 0.09375, ((0, 4), (1, 4)))
    taper_blocks = jnp.clip(jax.random.uniform(own_keys[2], (TX, TY, 5, S, S), jnp.float32, -0.03515625, 0.03515625) * level_of(own_keys[2], (TX, TY, 5, S, S), ((0, 4), (1, 4)), -0.4, 0.0), -0.03515625, 0.03515625).astype(jnp.bfloat16)
    taper_mask = set_ends((jax.random.randint(own_keys[3], (TX, TY, 5), 0, 8) < 7).astype(jnp.int32), jax.random.fold_in(own_keys[3], 1), 0, 1)
    nugget = jnp.clip(jnp.exp(math.log(6.0) - 1.3862944 * jax.random.uniform(own_keys[4], (TX, TY, S), jnp.float32) ** level_of(own_keys[4], (TX, TY, S), ((0, 4), (1, 4)), -0.2, 0.2)), 1.5, 6.0)
    return dict(probes=probes, lowrank_factor=lowrank_factor, taper_blocks=taper_blocks, taper_mask=taper_mask, nugget=nugget)


OFFSETS = ((0, 0), (0, 1), (-1, 0), (1, 1), (1, -1))
HIGH = lax.Precision.HIGHEST

def sparse_image(direction, blocks, taper_mask, nugget):
    narrow = direction.astype(jnp.bfloat16).astype(jnp.float32)
    tile_rows = narrow.shape[1]
    tile_cols = narrow.shape[2]
    masked = blocks.astype(jnp.float32) * taper_mask.astype(jnp.float32)[..., None, None]
    padded = jnp.pad(narrow, ((0, 0), (1, 1), (1, 1), (0, 0)))
    beside_all = jnp.stack([padded[:, 1 + step_row:1 + step_row + tile_rows, 1 + step_col:1 + step_col + tile_cols, :] for step_row, step_col in OFFSETS])
    forward = jnp.einsum('abost,okabt->kabs', masked, beside_all, precision=HIGH)
    backward = jnp.einsum('abost,kabs->okabt', masked, narrow, precision=HIGH)
    shifted = jnp.pad(backward[1:], ((0, 0), (0, 0), (1, 1), (1, 1), (0, 0)))
    summed = forward + backward[0]
    for position in range(4):
        step_row, step_col = OFFSETS[position + 1]
        summed = summed + shifted[position, :, 1 - step_row:1 - step_row + tile_rows, 1 - step_col:1 - step_col + tile_cols, :]
    return summed + nugget[None] * direction

def reference(probes, lowrank_factor, taper_blocks, taper_mask, nugget):
    count = probes.shape[0]
    width = lowrank_factor.shape[-1]
    factor_flat = lowrank_factor.reshape(-1, width)
    shape = probes.shape
    solution = jnp.zeros(shape, jnp.float32)
    remainder = probes
    direction = probes
    flat_rem = remainder.reshape(count, -1)
    gram_now = jnp.dot(flat_rem, flat_rem.T, precision=HIGH)
    projected = jnp.zeros((count, width), jnp.float32)
    probe_image = projected
    for sweep in range(ITERS):
        image = sparse_image(direction, taper_blocks, taper_mask, nugget)
        flat_dir = direction.reshape(count, -1)
        lowrank = jnp.dot(flat_dir.astype(jnp.bfloat16).astype(jnp.float32), factor_flat.astype(jnp.float32), preferred_element_type=jnp.float32)
        if sweep == 0:
            probe_image = lowrank
        curvature = jnp.dot(lowrank, lowrank.T, precision=HIGH) + jnp.dot(flat_dir, image.reshape(count, -1).T, precision=HIGH)
        image = image + jnp.dot(lowrank.astype(jnp.bfloat16).astype(jnp.float32), factor_flat.T.astype(jnp.float32), preferred_element_type=jnp.float32).reshape(shape)
        step_size = jnp.linalg.solve(curvature, gram_now)
        solution = solution + jnp.dot(step_size.T, flat_dir, precision=HIGH).reshape(shape)
        remainder = remainder - jnp.dot(step_size.T, image.reshape(count, -1), precision=HIGH).reshape(shape)
        projected = projected + jnp.dot(step_size.T, lowrank, precision=HIGH)
        if sweep + 1 < ITERS:
            flat_rem = remainder.reshape(count, -1)
            gram_next = jnp.dot(flat_rem, flat_rem.T, precision=HIGH)
            mixing = jnp.linalg.solve(gram_now, gram_next)
            direction = remainder + jnp.dot(mixing.T, flat_dir, precision=HIGH).reshape(shape)
            gram_now = gram_next
    gradient = (jnp.sum(projected * probe_image) / (count * width)).reshape(1)
    return (solution, remainder, gradient)
```

```python
import functools

import jax
import jax.numpy as jnp
from jax import lax
from jax.experimental import pallas as pl
from jax.experimental.pallas import tpu as pltpu
from jax.sharding import PartitionSpec as P

OFFSETS = ((0, 0), (0, 1), (-1, 0), (1, 1), (1, -1))
HIGH = lax.Precision.HIGHEST
F32 = jnp.float32
BF16 = jnp.bfloat16
CHUNK = 256
NT = (((1,), (1,)), ((), ()))
TN = (((0,), (0,)), ((), ()))
MESH = pl.DeviceIdType.MESH


def side(index, length):
    return -1 if index < 0 else (1 if index >= length else 0)


def halo_plan(rows, cols):
    sends = {}
    for r in range(rows):
        for c in range(cols):
            for o in range(1, 5):
                dr, dc = OFFSETS[o]
                for sign, item in ((-1, ("v", 0, r, c)), (1, ("c", o, r, c))):
                    way = (side(r + sign * dr, rows), side(c + sign * dc, cols))
                    if way != (0, 0) and item not in sends.setdefault(way, []):
                        sends[way].append(item)
    sends = {way: items for way, items in sorted(sends.items()) if items}
    base, total = {}, 0
    for way, items in sends.items():
        base[way] = total
        total += len(items)
    return sends, base, total


def high(a, b, dims):
    return lax.dot_general(a, b, dims, precision=HIGH, preferred_element_type=F32)


def eliminate(matrix, rights):
    size = matrix.shape[0]
    sub = lax.broadcasted_iota(jnp.int32, (size, 1), 0)
    for k in range(size):
        pivot = 1.0 / matrix[k : k + 1, k : k + 1]
        column = matrix[:, k : k + 1]

        def step(array):
            row = array[k : k + 1, :] * pivot
            return jnp.where(sub == k, row, array - column * row)

        rights = [step(right) for right in rights]
        matrix = step(matrix)
    return rights


def kernel(dims, x_ref, f_hbm, b_hbm, mask_ref, nug_ref, sol_ref, rem_ref, grad_ref,
           f_v, b_v, xb, part, own, rs_in, s2_out, s2_in, full, hal_out, hal_in, cprod, sm_out, sm_in, sm2_out, sm2_in,
           f_sem, b_sem, snd, rcv, hs, hr):
    nx, ny, rows, cols, count, width = dims
    tiles = rows * cols
    points = tiles * 128
    piece = width // nx
    pc = piece // CHUNK
    split = pc % ny == 0
    sc = pc // ny if split else pc
    i = lax.axis_index("sx")
    j = lax.axis_index("sy")
    sends, base, _ = halo_plan(rows, cols)
    ways = list(sends)

    def xp(d):
        return {"sx": lax.rem(i + d, nx)}

    def yp(d):
        return {"sy": lax.rem(j + d, ny)}

    def exists(way):
        a, b = i + way[0], j + way[1]
        return (a >= 0) & (a < nx) & (b >= 0) & (b < ny)

    def neighbour(way):
        return {"sx": i + way[0], "sy": j + way[1]}

    f_copies = []
    for d in range(1, nx + 1):
        p = lax.rem(i + d, nx)
        copy = pltpu.make_async_copy(
            f_hbm.at[:, pl.ds(pl.multiple_of(p * piece, piece), piece)], f_v.at[p], f_sem.at[d - 1])
        copy.start()
        f_copies.append(copy)
    b_copy = pltpu.make_async_copy(b_hbm, b_v, b_sem)
    b_copy.start()

    barrier = pltpu.get_barrier_semaphore()
    for d in range(1, nx):
        pl.semaphore_signal(barrier, inc=1, device_id=xp(d), device_id_type=MESH)
    for d in range(1, ny):
        pl.semaphore_signal(barrier, inc=1, device_id=yp(d), device_id_type=MESH)
    corners = [(a, b) for a in (-1, 1) for b in (-1, 1)]
    for way in corners:
        @pl.when(exists(way))
        def _():
            pl.semaphore_signal(barrier, inc=1, device_id=neighbour(way), device_id_type=MESH)
    near = sum(jnp.where(exists(way), 1, 0) for way in corners)
    pl.semaphore_wait(barrier, nx + ny - 2 + near)

    def remote(src, dst, it, slot, target):
        return pltpu.make_async_remote_copy(
            src_ref=src, dst_ref=dst, send_sem=snd.at[it, slot], recv_sem=rcv.at[it, slot],
            device_id=target, device_id_type=MESH)

    def image(it, x):
        narrow = x.astype(BF16)
        xb[it] = narrow
        pend = []
        slot = 0
        st1 = []
        for d in range(1, nx + 1):
            p = lax.rem(i + d, nx)
            if it == 0:
                f_copies[d - 1].wait()
            product = jnp.dot(xb[it], f_v[p], preferred_element_type=F32)
            for c in range(pc):
                piece_c = product[:, c * CHUNK : (c + 1) * CHUNK]
                if d < nx:
                    part[it, p, c] = piece_c.astype(BF16)
                else:
                    own[c] = piece_c
            if d < nx:
                copy = remote(part.at[it, p], rs_in.at[it, d - 1], it, slot, xp(d))
                copy.start()
                st1.append(copy)
                slot += 1
        if it == 0:
            b_copy.wait()

        def block(r, c, o):
            return b_v[pl.ds(((r * cols + c) * 5 + o) * 128, 128), :]

        def tile(r, c):
            t = r * cols + c
            return xb[it, :, t * 128 : (t + 1) * 128]

        def mask(r, c, o):
            return mask_ref[r, c, o].astype(F32)

        order = [(o, r, c) for o in range(1, 5) for r in range(rows) for c in range(cols)]
        for o, r, c in order:
            value = jnp.dot(tile(r, c), block(r, c, o), preferred_element_type=F32) * mask(r, c, o)
            cprod[it, (r * cols + c) * 4 + o - 1] = value.astype(BF16)
        halo = []
        for n, way in enumerate(ways):
            for k, (kind, o, r, c) in enumerate(sends[way]):
                hal_out[it, base[way] + k] = tile(r, c) if kind == "v" else cprod[it, (r * cols + c) * 4 + o - 1]
            span = pl.ds(base[way], len(sends[way]))
            copy = pltpu.make_async_remote_copy(
                src_ref=hal_out.at[it, span], dst_ref=hal_in.at[it, span], send_sem=hs.at[it, n], recv_sem=hr.at[it, n],
                device_id=neighbour(way), device_id_type=MESH)
            back = (-way[0], -way[1])
            halo.append((copy, way, back))

            @pl.when(exists(way))
            def _():
                copy.start()
        for copy in st1:
            copy.wait_recv()
        for c in range(pc):
            total = own[c]
            for d in range(1, nx):
                total = total + rs_in[it, d - 1, c].astype(F32)
            own[c] = total
            s2_out[it, c] = total.astype(BF16)
        st2 = []
        for d in range(1, ny):
            q = lax.rem(j + d, ny)
            src = s2_out.at[it, pl.ds(q * sc, sc)] if split else s2_out.at[it]
            dst = s2_in.at[it, d - 1] if split else s2_in.at[it, j]
            copy = remote(src, dst, it, slot, yp(d))
            copy.start()
            st2.append(copy)
            slot += 1
        for copy, way, back in halo:
            @pl.when(exists(back))
            def _():
                copy.wait_recv()

            @pl.when(jnp.logical_not(exists(back)))
            def _():
                span = pl.ds(base[way], len(sends[way]))
                hal_in[it, span] = jnp.zeros((len(sends[way]), count, 128), BF16)

        def arrived(kind, o, r, c):
            e = (side(r, rows), side(c, cols))
            if e == (0, 0):
                return tile(r, c) if kind == "v" else cprod[it, (r * cols + c) * 4 + o - 1]
            way = (-e[0], -e[1])
            return hal_in[it, base[way] + sends[way].index((kind, o, r - e[0] * rows, c - e[1] * cols))]

        image_tiles = []
        for r in range(rows):
            for c in range(cols):
                t = r * cols + c
                total = nug_ref[t : t + 1, :] * x[:, t * 128 : (t + 1) * 128]
                for o, (dr, dc) in enumerate(OFFSETS):
                    ahead = tile(r, c) if o == 0 else arrived("v", 0, r + dr, c + dc)
                    total = total + mask(r, c, o) * lax.dot_general(ahead, block(r, c, o), NT, preferred_element_type=F32)
                    if o == 0:
                        total = total + mask(r, c, 0) * jnp.dot(ahead, block(r, c, 0), preferred_element_type=F32)
                    else:
                        total = total + arrived("c", o, r - dr, c - dc).astype(F32)
                image_tiles.append(total)
        sparse = jnp.concatenate(image_tiles, axis=1)
        return sparse, slot, st1, st2, halo

    def finish(it, x, sparse, first, state):
        _, slot, st1, st2, halo = state
        for copy in st2:
            copy.wait_recv()
        st3 = []
        if split:
            for c in range(sc):
                total = own[j * sc + c]
                for d in range(1, ny):
                    total = total + s2_in[it, d - 1, c].astype(F32)
                full[it, i * pc + j * sc + c] = total.astype(BF16)
            for d in range(1, ny):
                span = pl.ds(i * pc + j * sc, sc)
                copy = remote(full.at[it, span], full.at[it, span], it, slot, yp(d))
                copy.start()
                st3.append(copy)
                slot += 1
        else:
            for c in range(pc):
                s2_in[it, j, c] = s2_out[it, c]
                total = s2_in[it, 0, c].astype(F32)
                for q in range(1, ny):
                    total = total + s2_in[it, q, c].astype(F32)
                full[it, i * pc + c] = total.astype(BF16)
        grams = high(x, jnp.concatenate([x, sparse, first, first], axis=0), NT)
        sm_out[it] = grams
        sm_in[it, i] = grams
        sm1 = []
        for d in range(1, nx):
            copy = remote(sm_out.at[it], sm_in.at[it, i], it, slot, xp(d))
            copy.start()
            sm1.append(copy)
            slot += 1
        for copy in st3:
            copy.wait_recv()
        st4 = []
        for d in range(1, nx):
            span = pl.ds(i * pc, pc)
            copy = remote(full.at[it, span], full.at[it, span], it, slot, xp(d))
            copy.start()
            st4.append(copy)
            slot += 1
        for copy in sm1:
            copy.wait_recv()
        total = sm_in[it, 0]
        for d in range(1, nx):
            total = total + sm_in[it, d]
        sm2_out[it] = total
        sm2_in[it, j] = total
        sm2 = []
        for d in range(1, ny):
            copy = remote(sm2_out.at[it], sm2_in.at[it, j], it, slot, yp(d))
            copy.start()
            sm2.append(copy)
            slot += 1
        image_total = sparse
        for d in range(nx):
            p = lax.rem(i - d + nx, nx)
            if d:
                st4[d - 1].wait_recv()
            for c in range(pc):
                image_total = image_total + lax.dot_general(
                    full[it, p * pc + c], f_v[p, :, c * CHUNK : (c + 1) * CHUNK], NT, preferred_element_type=F32)
        low = None
        for c in range(width // CHUNK):
            mine = full[it, c]
            both = mine if it == 0 else jnp.concatenate([full[0, c], mine], axis=0)
            term = lax.dot_general(mine, both, NT, preferred_element_type=F32)
            low = term if low is None else low + term
        for copy in sm2:
            copy.wait_recv()
        total = sm2_in[it, 0]
        for d in range(1, ny):
            total = total + sm2_in[it, d]
        for copy in st1 + st2 + st3 + sm1 + st4 + sm2:
            copy.wait_send()
        for copy, way, back in halo:
            @pl.when(exists(way))
            def _():
                copy.wait_send()
        return image_total, low, total

    n = count
    x0 = jnp.concatenate([x_ref[pl.ds(t, n, stride=tiles), :] for t in range(tiles)], axis=1)
    state = image(0, x0)
    y0 = state[0]
    w0, uu, small = finish(0, x0, y0, y0, state)
    g0 = small[:, :n]
    h0 = uu + small[:, n : 2 * n]
    (s0,) = eliminate(h0, [g0])
    r1 = x0 - high(s0, w0, TN)
    state = image(1, r1)
    y1 = state[0]
    t1, low, small = finish(1, r1, y1, y0, state)
    g1 = small[:, :n]
    rar = low[:, n : 2 * n] + small[:, n : 2 * n]
    rav = low[:, :n] + small[:, 2 * n : 3 * n]
    (m,) = eliminate(g0, [g1])
    half = high(rav, m, (((1,), (0,)), ((), ())))
    h1 = rar + half + half.T + high(m, high(h0, m, (((1,), (0,)), ((), ()))), TN)
    (s1,) = eliminate(h1, [g1])
    ms = high(m, s1, (((1,), (0,)), ((), ())))
    answer = high(s0 + ms, x0, TN) + high(s1, r1, TN)
    left = r1 - high(s1, t1, TN) - high(ms, w0, TN)
    for t in range(tiles):
        sol_ref[pl.ds(t, n, stride=tiles), :] = answer[:, t * 128 : (t + 1) * 128]
        rem_ref[pl.ds(t, n, stride=tiles), :] = left[:, t * 128 : (t + 1) * 128]
    trace = (s0 * uu + s1 * (low[:, :n] + high(m, uu, TN))) * (1.0 / (count * width))
    grad_ref[0] = jnp.sum(trace)


def local(nx, ny, probes, lowrank_factor, taper_blocks, taper_mask, nugget):
    count, rows, cols, span = probes.shape
    width = lowrank_factor.shape[-1]
    tiles = rows * cols
    points = tiles * span
    piece = width // nx
    pc = piece // CHUNK
    split = pc % ny == 0
    halo = halo_plan(rows, cols)
    slots = 3 * (nx - 1) + 3 * (ny - 1)
    vm = pltpu.VMEM
    dma = pltpu.SemaphoreType.DMA
    sc = pc // ny if split else pc
    answer, left, gradient = pl.pallas_call(
        functools.partial(kernel, (nx, ny, rows, cols, count, width)),
        out_shape=(
            jax.ShapeDtypeStruct((count * tiles, span), F32),
            jax.ShapeDtypeStruct((count * tiles, span), F32),
            jax.ShapeDtypeStruct((1,), F32),
        ),
        in_specs=[
            pl.BlockSpec(memory_space=vm),
            pl.BlockSpec(memory_space=pl.ANY),
            pl.BlockSpec(memory_space=pl.ANY),
            pl.BlockSpec(memory_space=pltpu.SMEM),
            pl.BlockSpec(memory_space=vm),
        ],
        out_specs=(
            pl.BlockSpec(memory_space=vm),
            pl.BlockSpec(memory_space=vm),
            pl.BlockSpec(memory_space=pltpu.SMEM),
        ),
        scratch_shapes=[
            vm((nx, points, piece), BF16),
            vm((tiles * 5 * span, span), BF16),
            vm((2, count, points), BF16),
            vm((2, nx, pc, count, CHUNK), BF16),
            vm((pc, count, CHUNK), F32),
            vm((2, nx - 1, pc, count, CHUNK), BF16),
            vm((2, pc, count, CHUNK), BF16),
            vm((2, ny - 1 if split else ny, sc, count, CHUNK), BF16),
            vm((2, width // CHUNK, count, CHUNK), BF16),
            vm((2, halo[2], count, span), BF16),
            vm((2, halo[2], count, span), BF16),
            vm((2, tiles * 4, count, span), BF16),
            vm((2, count, 4 * count), F32),
            vm((2, nx, count, 4 * count), F32),
            vm((2, count, 4 * count), F32),
            vm((2, ny, count, 4 * count), F32),
            dma((nx,)),
            dma,
            dma((2, slots)),
            dma((2, slots)),
            dma((2, len(halo[0]))),
            dma((2, len(halo[0]))),
        ],
        compiler_params=pltpu.CompilerParams(
            collective_id=0, has_side_effects=True, vmem_limit_bytes=48 * 1024 * 1024),
    )(
        probes.reshape(count * tiles, span),
        lowrank_factor.reshape(points, width),
        taper_blocks.reshape(tiles * 5 * span, span),
        taper_mask,
        nugget.reshape(tiles, span),
    )
    return answer.reshape(probes.shape), left.reshape(probes.shape), gradient


def solution(mesh):
    in_specs = (
        P("grp", "sx", "sy", None),
        P(("grp", "sx"), "sy", None, None),
        P(("grp", "sx"), "sy", None, None, None),
        P(("grp", "sx"), "sy", None),
        P(("grp", "sx"), "sy", None),
    )
    out_specs = (P("grp", "sx", "sy", None), P("grp", "sx", "sy", None), P("grp"))
    run = functools.partial(local, mesh.shape["sx"], mesh.shape["sy"])
    return jax.shard_map(run, mesh=mesh, in_specs=in_specs, out_specs=out_specs, check_vma=False)
```

```python
import functools

import jax
import jax.numpy as jnp
from jax import lax
from jax.experimental import pallas as pl
from jax.experimental.pallas import tpu as pltpu
from jax.sharding import PartitionSpec as P

OFFSETS = ((0, 0), (0, 1), (-1, 0), (1, 1), (1, -1))
HIGH = lax.Precision.HIGHEST
F32 = jnp.float32
BF16 = jnp.bfloat16
CHUNK = 256
NT = (((1,), (1,)), ((), ()))
TN = (((0,), (0,)), ((), ()))
MESH = pl.DeviceIdType.MESH


def side(index, length):
    return -1 if index < 0 else (1 if index >= length else 0)


def halo_plan(rows, cols):
    sends = {}
    for r in range(rows):
        for c in range(cols):
            for o in range(1, 5):
                dr, dc = OFFSETS[o]
                for sign, item in ((-1, ("v", 0, r, c)), (1, ("c", o, r, c))):
                    way = (side(r + sign * dr, rows), side(c + sign * dc, cols))
                    if way != (0, 0) and item not in sends.setdefault(way, []):
                        sends[way].append(item)
    sends = {way: items for way, items in sorted(sends.items()) if items}
    base, total = {}, 0
    for way, items in sends.items():
        base[way] = total
        total += len(items)
    return sends, base, total


def high(a, b, dims):
    return lax.dot_general(a, b, dims, precision=HIGH, preferred_element_type=F32)


def eliminate(systems):
    size = systems[0][0].shape[0]
    sub = lax.broadcasted_iota(jnp.int32, (size, 1), 0)
    for k in range(size):
        following = []
        for matrix, right in systems:
            pivot = 1.0 / matrix[k : k + 1, k : k + 1]
            column = matrix[:, k : k + 1]
            rows = [array[k : k + 1, :] * pivot for array in (matrix, right)]
            following.append(tuple(
                jnp.where(sub == k, row, array - column * row) for array, row in zip((matrix, right), rows)))
        systems = following
    return [right for _, right in systems]


def kernel(dims, x_ref, f_hbm, b_hbm, mask_ref, nug_ref, sol_ref, rem_ref, grad_ref,
           f_v, b_v, xb, part, own, rs_in, s2_out, s2_in, full, hal_out, hal_in, cprod, sm_out, sm_in, sm2_out, sm2_in,
           f_sem, b_sem, snd, rcv, hs, hr):
    nx, ny, rows, cols, count, width = dims
    tiles = rows * cols
    points = tiles * 128
    piece = width // nx
    pc = piece // CHUNK
    split = pc % ny == 0
    sc = pc // ny if split else pc
    i = lax.axis_index("sx")
    j = lax.axis_index("sy")
    sends, base, _ = halo_plan(rows, cols)
    ways = list(sends)

    def xp(d):
        return {"sx": lax.rem(i + d, nx)}

    def yp(d):
        return {"sy": lax.rem(j + d, ny)}

    def exists(way):
        a, b = i + way[0], j + way[1]
        return (a >= 0) & (a < nx) & (b >= 0) & (b < ny)

    def neighbour(way):
        return {"sx": i + way[0], "sy": j + way[1]}

    f_copies = []
    for d in range(1, nx + 1):
        p = lax.rem(i + d, nx)
        copy = pltpu.make_async_copy(
            f_hbm.at[:, pl.ds(pl.multiple_of(p * piece, piece), piece)], f_v.at[p], f_sem.at[d - 1])
        copy.start()
        f_copies.append(copy)
    b_copy = pltpu.make_async_copy(b_hbm, b_v, b_sem)
    b_copy.start()

    barrier = pltpu.get_barrier_semaphore()
    for d in range(1, nx):
        pl.semaphore_signal(barrier, inc=1, device_id=xp(d), device_id_type=MESH)
    for d in range(1, ny):
        pl.semaphore_signal(barrier, inc=1, device_id=yp(d), device_id_type=MESH)
    corners = [(a, b) for a in (-1, 1) for b in (-1, 1)]
    for way in corners:
        @pl.when(exists(way))
        def _():
            pl.semaphore_signal(barrier, inc=1, device_id=neighbour(way), device_id_type=MESH)
    near = sum(jnp.where(exists(way), 1, 0) for way in corners)
    pl.semaphore_wait(barrier, nx + ny - 2 + near)

    def remote(src, dst, it, slot, target):
        return pltpu.make_async_remote_copy(
            src_ref=src, dst_ref=dst, send_sem=snd.at[it, slot], recv_sem=rcv.at[it, slot],
            device_id=target, device_id_type=MESH)

    def image(it, x):
        narrow = x.astype(BF16)
        xb[it] = narrow
        pend = []
        slot = 0
        st1 = []
        for d in range(1, nx + 1):
            p = lax.rem(i + d, nx)
            if it == 0:
                f_copies[d - 1].wait()
            product = jnp.dot(xb[it], f_v[p], preferred_element_type=F32)
            for c in range(pc):
                piece_c = product[:, c * CHUNK : (c + 1) * CHUNK]
                if d < nx:
                    part[it, p, c] = piece_c.astype(BF16)
                else:
                    own[c] = piece_c
            if d < nx:
                copy = remote(part.at[it, p], rs_in.at[it, d - 1], it, slot, xp(d))
                copy.start()
                st1.append(copy)
                slot += 1
        if it == 0:
            b_copy.wait()

        def block(r, c, o):
            return b_v[pl.ds(((r * cols + c) * 5 + o) * 128, 128), :]

        def tile(r, c):
            t = r * cols + c
            return xb[it, :, t * 128 : (t + 1) * 128]

        def mask(r, c, o):
            return mask_ref[r, c, o].astype(F32)

        order = [(o, r, c) for o in range(1, 5) for r in range(rows) for c in range(cols)]
        for o, r, c in order:
            value = jnp.dot(tile(r, c), block(r, c, o), preferred_element_type=F32) * mask(r, c, o)
            cprod[it, (r * cols + c) * 4 + o - 1] = value.astype(BF16)
        halo = []
        for n, way in enumerate(ways):
            for k, (kind, o, r, c) in enumerate(sends[way]):
                hal_out[it, base[way] + k] = tile(r, c) if kind == "v" else cprod[it, (r * cols + c) * 4 + o - 1]
            span = pl.ds(base[way], len(sends[way]))
            copy = pltpu.make_async_remote_copy(
                src_ref=hal_out.at[it, span], dst_ref=hal_in.at[it, span], send_sem=hs.at[it, n], recv_sem=hr.at[it, n],
                device_id=neighbour(way), device_id_type=MESH)
            back = (-way[0], -way[1])
            halo.append((copy, way, back))

            @pl.when(exists(way))
            def _():
                copy.start()
        for copy in st1:
            copy.wait_recv()
        for c in range(pc):
            total = own[c]
            for d in range(1, nx):
                total = total + rs_in[it, d - 1, c].astype(F32)
            own[c] = total
            s2_out[it, c] = total.astype(BF16)
        st2 = []
        for d in range(1, ny):
            q = lax.rem(j + d, ny)
            src = s2_out.at[it, pl.ds(q * sc, sc)] if split else s2_out.at[it]
            dst = s2_in.at[it, d - 1] if split else s2_in.at[it, j]
            copy = remote(src, dst, it, slot, yp(d))
            copy.start()
            st2.append(copy)
            slot += 1
        for copy, way, back in halo:
            @pl.when(exists(back))
            def _():
                copy.wait_recv()

            @pl.when(jnp.logical_not(exists(back)))
            def _():
                span = pl.ds(base[way], len(sends[way]))
                hal_in[it, span] = jnp.zeros((len(sends[way]), count, 128), BF16)

        def arrived(kind, o, r, c):
            e = (side(r, rows), side(c, cols))
            if e == (0, 0):
                return tile(r, c) if kind == "v" else cprod[it, (r * cols + c) * 4 + o - 1]
            way = (-e[0], -e[1])
            return hal_in[it, base[way] + sends[way].index((kind, o, r - e[0] * rows, c - e[1] * cols))]

        image_tiles = []
        for r in range(rows):
            for c in range(cols):
                t = r * cols + c
                total = nug_ref[t : t + 1, :] * x[:, t * 128 : (t + 1) * 128]
                for o, (dr, dc) in enumerate(OFFSETS):
                    ahead = tile(r, c) if o == 0 else arrived("v", 0, r + dr, c + dc)
                    total = total + mask(r, c, o) * lax.dot_general(ahead, block(r, c, o), NT, preferred_element_type=F32)
                    if o == 0:
                        total = total + mask(r, c, 0) * jnp.dot(ahead, block(r, c, 0), preferred_element_type=F32)
                    else:
                        total = total + arrived("c", o, r - dr, c - dc).astype(F32)
                image_tiles.append(total)
        sparse = jnp.concatenate(image_tiles, axis=1)
        return sparse, slot, st1, st2, halo

    def finish(it, x, sparse, first, state):
        _, slot, st1, st2, halo = state
        for copy in st2:
            copy.wait_recv()
        st3 = []
        if split:
            for c in range(sc):
                total = own[j * sc + c]
                for d in range(1, ny):
                    total = total + s2_in[it, d - 1, c].astype(F32)
                full[it, i * pc + j * sc + c] = total.astype(BF16)
            for d in range(1, ny):
                span = pl.ds(i * pc + j * sc, sc)
                copy = remote(full.at[it, span], full.at[it, span], it, slot, yp(d))
                copy.start()
                st3.append(copy)
                slot += 1
        else:
            for c in range(pc):
                s2_in[it, j, c] = s2_out[it, c]
                total = s2_in[it, 0, c].astype(F32)
                for q in range(1, ny):
                    total = total + s2_in[it, q, c].astype(F32)
                full[it, i * pc + c] = total.astype(BF16)
        grams = high(x, jnp.concatenate([x, sparse, first, first], axis=0), NT)
        sm_out[it] = grams
        sm_in[it, i] = grams
        sm1 = []
        for d in range(1, nx):
            copy = remote(sm_out.at[it], sm_in.at[it, i], it, slot, xp(d))
            copy.start()
            sm1.append(copy)
            slot += 1
        for copy in st3:
            copy.wait_recv()
        st4 = []
        for d in range(1, nx):
            span = pl.ds(i * pc, pc)
            copy = remote(full.at[it, span], full.at[it, span], it, slot, xp(d))
            copy.start()
            st4.append(copy)
            slot += 1
        for copy in sm1:
            copy.wait_recv()
        total = sm_in[it, 0]
        for d in range(1, nx):
            total = total + sm_in[it, d]
        sm2_out[it] = total
        sm2_in[it, j] = total
        sm2 = []
        for d in range(1, ny):
            copy = remote(sm2_out.at[it], sm2_in.at[it, j], it, slot, yp(d))
            copy.start()
            sm2.append(copy)
            slot += 1
        image_total = sparse
        for d in range(nx):
            p = lax.rem(i - d + nx, nx)
            if d:
                st4[d - 1].wait_recv()
            for c in range(pc):
                image_total = image_total + lax.dot_general(
                    full[it, p * pc + c], f_v[p, :, c * CHUNK : (c + 1) * CHUNK], NT, preferred_element_type=F32)
        low = None
        for c in range(width // CHUNK):
            mine = full[it, c]
            both = mine if it == 0 else jnp.concatenate([full[0, c], mine], axis=0)
            term = lax.dot_general(mine, both, NT, preferred_element_type=F32)
            low = term if low is None else low + term
        for copy in sm2:
            copy.wait_recv()
        total = sm2_in[it, 0]
        for d in range(1, ny):
            total = total + sm2_in[it, d]
        for copy in st1 + st2 + st3 + sm1 + st4 + sm2:
            copy.wait_send()
        for copy, way, back in halo:
            @pl.when(exists(way))
            def _():
                copy.wait_send()
        return image_total, low, total

    n = count
    x0 = jnp.concatenate([x_ref[pl.ds(t, n, stride=tiles), :] for t in range(tiles)], axis=1)
    state = image(0, x0)
    y0 = state[0]
    w0, uu, small = finish(0, x0, y0, y0, state)
    g0 = small[:, :n]
    h0 = uu + small[:, n : 2 * n]
    eye = jnp.where(
        lax.broadcasted_iota(jnp.int32, (n, n), 0) == lax.broadcasted_iota(jnp.int32, (n, n), 1), 1.0, 0.0)
    s0, g0_inverse = eliminate([(h0, g0), (g0, eye)])
    r1 = x0 - high(s0, w0, TN)
    state = image(1, r1)
    y1 = state[0]
    t1, low, small = finish(1, r1, y1, y0, state)
    g1 = small[:, :n]
    rar = low[:, n : 2 * n] + small[:, n : 2 * n]
    rav = low[:, :n] + small[:, 2 * n : 3 * n]
    m = high(g0_inverse, g1, (((1,), (0,)), ((), ())))
    half = high(rav, m, (((1,), (0,)), ((), ())))
    h1 = rar + half + half.T + high(m, high(h0, m, (((1,), (0,)), ((), ()))), TN)
    (s1,) = eliminate([(h1, g1)])
    ms = high(m, s1, (((1,), (0,)), ((), ())))
    answer = high(s0 + ms, x0, TN) + high(s1, r1, TN)
    left = r1 - high(s1, t1, TN) - high(ms, w0, TN)
    for t in range(tiles):
        sol_ref[pl.ds(t, n, stride=tiles), :] = answer[:, t * 128 : (t + 1) * 128]
        rem_ref[pl.ds(t, n, stride=tiles), :] = left[:, t * 128 : (t + 1) * 128]
    trace = (s0 * uu + s1 * (low[:, :n] + high(m, uu, TN))) * (1.0 / (count * width))
    grad_ref[0] = jnp.sum(trace)


def local(nx, ny, probes, lowrank_factor, taper_blocks, taper_mask, nugget):
    count, rows, cols, span = probes.shape
    width = lowrank_factor.shape[-1]
    tiles = rows * cols
    points = tiles * span
    piece = width // nx
    pc = piece // CHUNK
    split = pc % ny == 0
    halo = halo_plan(rows, cols)
    slots = 3 * (nx - 1) + 3 * (ny - 1)
    vm = pltpu.VMEM
    dma = pltpu.SemaphoreType.DMA
    sc = pc // ny if split else pc
    answer, left, gradient = pl.pallas_call(
        functools.partial(kernel, (nx, ny, rows, cols, count, width)),
        out_shape=(
            jax.ShapeDtypeStruct((count * tiles, span), F32),
            jax.ShapeDtypeStruct((count * tiles, span), F32),
            jax.ShapeDtypeStruct((1,), F32),
        ),
        in_specs=[
            pl.BlockSpec(memory_space=vm),
            pl.BlockSpec(memory_space=pl.ANY),
            pl.BlockSpec(memory_space=pl.ANY),
            pl.BlockSpec(memory_space=pltpu.SMEM),
            pl.BlockSpec(memory_space=vm),
        ],
        out_specs=(
            pl.BlockSpec(memory_space=vm),
            pl.BlockSpec(memory_space=vm),
            pl.BlockSpec(memory_space=pltpu.SMEM),
        ),
        scratch_shapes=[
            vm((nx, points, piece), BF16),
            vm((tiles * 5 * span, span), BF16),
            vm((2, count, points), BF16),
            vm((2, nx, pc, count, CHUNK), BF16),
            vm((pc, count, CHUNK), F32),
            vm((2, nx - 1, pc, count, CHUNK), BF16),
            vm((2, pc, count, CHUNK), BF16),
            vm((2, ny - 1 if split else ny, sc, count, CHUNK), BF16),
            vm((2, width // CHUNK, count, CHUNK), BF16),
            vm((2, halo[2], count, span), BF16),
            vm((2, halo[2], count, span), BF16),
            vm((2, tiles * 4, count, span), BF16),
            vm((2, count, 4 * count), F32),
            vm((2, nx, count, 4 * count), F32),
            vm((2, count, 4 * count), F32),
            vm((2, ny, count, 4 * count), F32),
            dma((nx,)),
            dma,
            dma((2, slots)),
            dma((2, slots)),
            dma((2, len(halo[0]))),
            dma((2, len(halo[0]))),
        ],
        compiler_params=pltpu.CompilerParams(
            collective_id=0, has_side_effects=True, vmem_limit_bytes=63 * 1024 * 1024),
    )(
        probes.reshape(count * tiles, span),
        lowrank_factor.reshape(points, width),
        taper_blocks.reshape(tiles * 5 * span, span),
        taper_mask,
        nugget.reshape(tiles, span),
    )
    return answer.reshape(probes.shape), left.reshape(probes.shape), gradient


def solution(mesh):
    in_specs = (
        P("grp", "sx", "sy", None),
        P(("grp", "sx"), "sy", None, None),
        P(("grp", "sx"), "sy", None, None, None),
        P(("grp", "sx"), "sy", None),
        P(("grp", "sx"), "sy", None),
    )
    out_specs = (P("grp", "sx", "sy", None), P("grp", "sx", "sy", None), P("grp"))
    run = functools.partial(local, mesh.shape["sx"], mesh.shape["sy"])
    return jax.shard_map(run, mesh=mesh, in_specs=in_specs, out_specs=out_specs, check_vma=False)
```
